256 devices in a mesh: rows: 256 (over z, y, x, core).
Axes of the slice: x: 4, y: 4, z: 8, core: 2. Of those that a mesh axis runs over, the one named last changes fastest.
Arguments:
- vectors: bfloat16 [16, 32, 65536], P(None, None, 'rows'), may hold values from -6 to 6
- factors: bfloat16 [10, 64, 64, 32768], P(None, None, None, 'rows'), may hold values from -0.75 to 0.75
- neighbor_blocks: bfloat16 [3, 32, 32, 65536], P(None, None, None, 'rows'), may hold values from -0.625 to 0.625
Outputs:
- product: bfloat16 [16, 32, 65536], P(None, None, 'rows')
The draws below stay inside these ranges and needn't reach their ends.
All inputs are finite; a program needn't handle non-finite values.
Results may differ from the reference program's by a relative error of at most 0.0094.
Values may be sent and summed in bfloat16 or wider, within the bound.
No kernel may reach another device: no remote copies, remote signals or barrier semaphores. Data moves between devices by JAX's collectives and lax.ppermute only.
A program may use at most 128 MiB of HBM per device.

```python
import jax
import jax.numpy as jnp

RHS = 16
BLOCK = 32
NB = 256
HALF = 128
COLS = 65536
DEPTH = 8
N_ROWS = 256


def levels(key, extent, cuts, least, largest):
    level = 1.0
    for axis_at, parts in cuts:
        steps = jax.random.uniform(jax.random.fold_in(jax.random.fold_in(key, 6), axis_at), (parts,), jnp.float32, least / len(cuts), largest / len(cuts))
        level = level * jnp.repeat(jnp.exp(steps), extent[axis_at] // parts).reshape((-1,) + (1,) * (len(extent) - 1 - axis_at))
    return level


def noise(key, shape, scale, bound, split=(), dtype=jnp.bfloat16):
    factor_of = levels(key, shape, split, -0.22, 0.18) if split else 1.0
    drawn = jax.random.normal(key, shape, jnp.float32) * scale * factor_of
    return jnp.minimum(jnp.maximum(drawn, -bound), bound).astype(dtype)


def setup_inputs(seed: int = 0) -> dict:
    key_of = jax.random.split(jax.random.key(seed), 4)
    return {
        "vectors": noise(key_of[0], (RHS, BLOCK, COLS), 1.0, 6.0, ((2, 256),)),
        "factors": noise(key_of[1], (DEPTH + 2, 2 * BLOCK, 2 * BLOCK, HALF * N_ROWS), (2 * BLOCK) ** -0.5, 0.75, ((3, 256),)),
        "neighbor_blocks": noise(key_of[2], (3, BLOCK, BLOCK, COLS), (3 * BLOCK) ** -0.5, 0.625, ((3, 256),)),
    }


def stacked_local(coeffs):
    grouped = coeffs.reshape(RHS, BLOCK, N_ROWS, 2, HALF)
    return grouped.transpose(0, 3, 1, 2, 4).reshape(RHS, 2 * BLOCK, N_ROWS, HALF)


def stacked_pairs(coeffs, level_index):
    stride = 2 ** level_index
    grouped = coeffs.reshape(RHS, BLOCK, N_ROWS // (2 * stride), 2, stride, 2, HALF)
    return grouped.transpose(0, 3, 1, 2, 5, 4, 6).reshape(RHS, 2 * BLOCK, N_ROWS, HALF)


def section_mix(weights, stacked):
    wide = weights.astype(jnp.float32).reshape(2 * BLOCK, 2 * BLOCK, N_ROWS, HALF)
    mixed = jnp.einsum('kjdg,sjdg->skdg', wide, stacked.astype(jnp.float32))
    mixed = mixed.reshape(RHS, 2, BLOCK, N_ROWS, HALF).transpose(0, 2, 3, 1, 4)
    return mixed.reshape(RHS, BLOCK, NB * N_ROWS)


def reference(vectors, factors, neighbor_blocks):
    coeffs = section_mix(factors[0], stacked_local(vectors)).astype(jnp.bfloat16)
    for level_index in range(DEPTH):
        coeffs = section_mix(factors[level_index + 1], stacked_pairs(coeffs, level_index)).astype(jnp.bfloat16)
    far_field = section_mix(factors[DEPTH + 1], stacked_local(coeffs))
    wide_near = neighbor_blocks.astype(jnp.float32)
    values = vectors.astype(jnp.float32)
    zero_block = jnp.zeros((RHS, BLOCK, 1), jnp.float32)
    before = jnp.concatenate([zero_block, values[:, :, :-1]], axis=2)
    after = jnp.concatenate([values[:, :, 1:], zero_block], axis=2)
    near_field = jnp.einsum('abk,sbk->sak', wide_near[0], values)
    near_field = near_field + jnp.einsum('abk,sbk->sak', wide_near[1], before)
    near_field = near_field + jnp.einsum('abk,sbk->sak', wide_near[2], after)
    return (far_field + near_field).astype(jnp.bfloat16)
```

```python
import functools

import jax
import jax.numpy as jnp
from jax import lax
from jax.experimental import pallas as pl
from jax.experimental.pallas import tpu as pltpu
from jax.sharding import PartitionSpec as P

RHS = 16
RANK = 32
HALF = 128
QUADS = 32
LANES = 128
BF16 = jnp.bfloat16
F32 = jnp.float32


def lane_bit(shape, step, dtype=jnp.int32):
    return (lax.broadcasted_iota(dtype, shape, len(shape) - 1) & step) != 0


def swap_major_lanes(blocks):
    blocks = list(blocks)
    shape = blocks[0].shape
    for step in (16, 8, 4, 2, 1):
        upper = lane_bit(shape, step)
        for low in range(QUADS):
            if low & step:
                continue
            high = low + step
            first, second = blocks[low], blocks[high]
            blocks[low] = jnp.where(upper, pltpu.roll(second, step, 1), first)
            blocks[high] = jnp.where(upper, second, pltpu.roll(first, LANES - step, 1))
    return blocks


def arrange_section(weights_ref, arranged_ref):
    for half in range(2):
        for rows in range(0, 2 * RANK, 16):
            blocks = [weights_ref[half * RANK + a, rows : rows + 16, :] for a in range(RANK)]
            for q, block in enumerate(swap_major_lanes(blocks)):
                arranged_ref[q, half, rows : rows + 16, :] = block


def diagonal_blocks(block, group):
    lane = lax.broadcasted_iota(jnp.int32, block.shape, 1)
    return jnp.where((lane >> 5) & 3 == group, block, jnp.zeros_like(block))


def section_quad(arranged_ref, q, lower, higher):
    tiles = []
    for half in range(2):
        rows = slice(half * RANK, (half + 1) * RANK)
        dense = jnp.concatenate([arranged_ref[q, 0, rows, :], arranged_ref[q, 1, rows, :]], axis=1)
        tiles += [diagonal_blocks(dense, group) for group in range(4)]
    matrix = jnp.concatenate(tiles, axis=0)
    stack = jnp.concatenate([lower, higher], axis=1)
    return jnp.dot(stack, matrix, preferred_element_type=F32)


def emit_halves(mixed, q, upper, own_ref, send_ref):
    first, second = mixed[:, :LANES], mixed[:, LANES:]
    own_ref[q] = jnp.where(upper, second, first)
    send_ref[q] = jnp.where(upper, first, second)


def level_bit(level):
    return (lax.axis_index("rows") >> level) & 1 == 1


def head_kernel(vectors_ref, weights_ref, own_ref, send_ref, halves_ref, rows_ref, arranged_ref):
    arrange_section(weights_ref.at[0], arranged_ref)
    for half in range(2):
        lanes = slice(half * HALF, (half + 1) * HALF)
        for r in range(RHS):
            rows_ref[r * RANK : (r + 1) * RANK, :] = vectors_ref[r, :, lanes].astype(F32)
        blocks = [rows_ref[pl.ds(a, RHS, stride=RANK), :].astype(BF16) for a in range(RANK)]
        for q, block in enumerate(swap_major_lanes(blocks)):
            halves_ref[half, q] = block
    upper = level_bit(0)
    for q in range(QUADS):
        mixed = section_quad(arranged_ref, q, halves_ref[0, q], halves_ref[1, q]).astype(BF16)
        emit_halves(mixed, q, upper, own_ref, send_ref)


def arrange_kernel(weights_ref, after_ref, arranged_ref):
    del after_ref
    arrange_section(weights_ref.at[0], arranged_ref)


def level_kernel(level, last, arranged_ref, kept_ref, received_ref, own_ref, send_ref):
    upper = level_bit(level)
    next_upper = False if last else level_bit(level + 1)
    for q in range(QUADS):
        kept, received = kept_ref[q], received_ref[q]
        lower = jnp.where(upper, received, kept)
        higher = jnp.where(upper, kept, received)
        mixed = section_quad(arranged_ref, q, lower, higher).astype(BF16)
        emit_halves(mixed, q, next_upper, own_ref, send_ref)


def near_kernel(halves_ref, before_ref, after_ref, blocks_ref, near_ref, arranged_ref):
    group = lax.broadcasted_iota(jnp.int32, (RHS, LANES), 1) >> 5
    for half in range(2):
        for shift in range(3):
            for rows in range(0, RANK, 16):
                lanes = slice(half * HALF, (half + 1) * HALF)
                blocks = [blocks_ref[shift, a, rows : rows + 16, lanes] for a in range(RANK)]
                for q, block in enumerate(swap_major_lanes(blocks)):
                    arranged_ref[shift, q, rows : rows + 16, :] = block
        edge_before = before_ref[...] if half == 0 else halves_ref[0, QUADS - 1]
        edge_after = after_ref[...] if half == 1 else halves_ref[1, 0]
        for q in range(QUADS):
            centre = halves_ref[half, q]
            if q > 0:
                before = halves_ref[half, q - 1]
            else:
                last = halves_ref[half, QUADS - 1]
                before = pltpu.roll(jnp.where(group == 3, edge_before, last), RANK, 1)
            if q < QUADS - 1:
                after = halves_ref[half, q + 1]
            else:
                first = halves_ref[half, 0]
                after = pltpu.roll(jnp.where(group == 0, edge_after, first), LANES - RANK, 1)
            tiles = [
                diagonal_blocks(arranged_ref[shift, q], part) for shift in range(3) for part in range(4)
            ]
            matrix = jnp.concatenate(tiles, axis=0)
            stack = jnp.concatenate([centre, before, after], axis=1)
            near_ref[half, q] = jnp.dot(stack, matrix, preferred_element_type=F32)


def root_kernel(arranged_ref, first_ref, second_ref, near_ref, product_ref, rows_ref):
    blocks = [[], []]
    for q in range(QUADS):
        mixed = section_quad(arranged_ref, q, first_ref[q], second_ref[q])
        for half in range(2):
            total = mixed[:, half * LANES : (half + 1) * LANES] + near_ref[half, q]
            blocks[half].append(total.astype(BF16))
    for half in range(2):
        lanes = slice(half * HALF, (half + 1) * HALF)
        for a, block in enumerate(swap_major_lanes(blocks[half])):
            rows_ref[half, a * RHS : (a + 1) * RHS, :] = block.astype(F32)
        for r in range(RHS):
            product_ref[r, :, lanes] = rows_ref[half, pl.ds(r, RANK, stride=RHS), :].astype(BF16)


VMEM_SPEC = pl.BlockSpec(memory_space=pltpu.VMEM)
ANY_SPEC = pl.BlockSpec(memory_space=pl.ANY)
PAYLOAD = jax.ShapeDtypeStruct((QUADS, RHS, LANES), BF16)
ARRANGED = (QUADS, 2, 2 * RANK, LANES)


def one_section(index):
    return pl.BlockSpec((1, 2 * RANK, 2 * RANK, HALF), lambda step: (index, 0, 0, 0))


def whole(shape):
    return pl.BlockSpec(shape, lambda step: (0,) * len(shape))


def params(mib):
    return pltpu.CompilerParams(vmem_limit_bytes=mib * 2**20)


def arrange(factors, index, after):
    return pl.pallas_call(
        arrange_kernel,
        grid=(1,),
        out_shape=jax.ShapeDtypeStruct(ARRANGED, BF16),
        in_specs=[one_section(index), ANY_SPEC],
        out_specs=whole(ARRANGED),
        compiler_params=params(8),
        cost_estimate=pl.CostEstimate(flops=2 * 10**6, bytes_accessed=2 * 2**20, transcendentals=0),
        name="arrange",
    )(factors, after)


def head(vectors, factors):
    return pl.pallas_call(
        head_kernel,
        grid=(1,),
        out_shape=(PAYLOAD, PAYLOAD, jax.ShapeDtypeStruct((2, QUADS, RHS, LANES), BF16)),
        in_specs=[whole((RHS, RANK, 2 * HALF)), one_section(0)],
        out_specs=(whole(PAYLOAD.shape), whole(PAYLOAD.shape), whole((2, QUADS, RHS, LANES))),
        scratch_shapes=[pltpu.VMEM((RHS * RANK, LANES), F32), pltpu.VMEM(ARRANGED, BF16)],
        compiler_params=params(12),
        name="head",
    )(vectors, factors)


def level_step(level, last, arranged, kept, received):
    return pl.pallas_call(
        functools.partial(level_kernel, level, last),
        out_shape=(PAYLOAD, PAYLOAD),
        in_specs=[VMEM_SPEC] * 3,
        out_specs=(VMEM_SPEC, VMEM_SPEC),
        compiler_params=params(6),
        name="level",
    )(arranged, kept, received)


def near_field(halves, before, after, neighbor_blocks):
    return pl.pallas_call(
        near_kernel,
        out_shape=jax.ShapeDtypeStruct((2, QUADS, RHS, LANES), F32),
        in_specs=[VMEM_SPEC] * 4,
        out_specs=VMEM_SPEC,
        scratch_shapes=[pltpu.VMEM((3, QUADS, RANK, LANES), BF16)],
        compiler_params=params(12),
        cost_estimate=pl.CostEstimate(flops=4 * 10**6, bytes_accessed=3 * 2**20, transcendentals=0),
        name="near",
    )(halves, before, after, neighbor_blocks)


def root(arranged, first, second, near):
    return pl.pallas_call(
        root_kernel,
        out_shape=jax.ShapeDtypeStruct((RHS, RANK, 2 * HALF), BF16),
        in_specs=[VMEM_SPEC] * 4,
        out_specs=VMEM_SPEC,
        scratch_shapes=[pltpu.VMEM((2, RHS * RANK, LANES), F32)],
        compiler_params=params(12),
        name="root",
    )(arranged, first, second, near)


def shards(vectors, factors, neighbor_blocks):
    level_count = factors.shape[0] - 2
    count = lax.axis_size("rows")
    kept, sending, halves = head(vectors, factors)
    before = lax.ppermute(halves[1, QUADS - 1], "rows", [(i, i + 1) for i in range(count - 1)])
    after = lax.ppermute(halves[0, 0], "rows", [(i + 1, i) for i in range(count - 1)])
    near = near_field(halves, before, after, neighbor_blocks)
    for level in range(level_count):
        received = lax.ppermute(sending, "rows", [(i, i ^ (1 << level)) for i in range(count)])
        arranged = arrange(factors, level + 1, sending)
        kept, sending = level_step(level, level == level_count - 1, arranged, kept, received)
    arranged = arrange(factors, level_count + 1, received)
    return root(arranged, kept, sending, near)


def solution(mesh):
    placed = (P(None, None, "rows"), P(None, None, None, "rows"), P(None, None, None, "rows"))
    return jax.shard_map(
        shards, mesh=mesh, in_specs=placed, out_specs=P(None, None, "rows"), check_vma=False
    )
```

```python
import functools

import jax
import jax.numpy as jnp
from jax import lax
from jax.experimental import pallas as pl
from jax.experimental.pallas import tpu as pltpu
from jax.sharding import PartitionSpec as P

RHS = 16
RANK = 32
HALF = 128
QUADS = 32
LANES = 128
PITCH = LANES + 1
CHAINS = 2
SLOTS = QUADS // CHAINS
PIECES = 4
NEAR_LEVEL = 2
BF16 = jnp.bfloat16
F32 = jnp.float32


def lane_bit(shape, step, dtype=jnp.int32):
    return (lax.broadcasted_iota(dtype, shape, len(shape) - 1) & step) != 0


def swap_major_lanes(blocks):
    blocks = list(blocks)
    shape = blocks[0].shape
    for step in (16, 8, 4, 2, 1):
        upper = lane_bit(shape, step)
        for low in range(QUADS):
            if low & step:
                continue
            high = low + step
            first, second = blocks[low], blocks[high]
            blocks[low] = jnp.where(upper, pltpu.roll(second, step, 1), first)
            blocks[high] = jnp.where(upper, second, pltpu.roll(first, LANES - step, 1))
    return blocks


def arrange_section(weights_ref, arranged_ref, turned_ref):
    for a in range(RANK):
        both = jnp.concatenate([weights_ref[a], weights_ref[RANK + a]], axis=0)
        turned_ref[a * PITCH : a * PITCH + LANES, :] = both.T.astype(F32)
    for q in range(QUADS):
        rows = [turned_ref[pl.ds(part * QUADS + q, RANK, stride=PITCH), :] for part in range(4)]
        turned = jnp.concatenate(rows, axis=0).astype(BF16).T
        arranged_ref[q] = turned.reshape(2, 2 * RANK, LANES)


def diagonal_blocks(block, group):
    lane = lax.broadcasted_iota(jnp.int32, block.shape, 1)
    return jnp.where((lane >> 5) & 3 == group, block, jnp.zeros_like(block))


def section_quad(arranged_ref, q, lower, higher):
    tiles = []
    for half in range(2):
        rows = slice(half * RANK, (half + 1) * RANK)
        dense = jnp.concatenate([arranged_ref[q, 0, rows, :], arranged_ref[q, 1, rows, :]], axis=1)
        tiles += [diagonal_blocks(dense, group) for group in range(4)]
    matrix = jnp.concatenate(tiles, axis=0)
    stack = jnp.concatenate([lower, higher], axis=1)
    return jnp.dot(stack, matrix, preferred_element_type=F32)


def emit_halves(mixed, q, upper, own_ref, send_ref):
    first, second = mixed[:, :LANES], mixed[:, LANES:]
    own_ref[q] = jnp.where(upper, second, first)
    send_ref[q] = jnp.where(upper, first, second)


def level_bit(level):
    return (lax.axis_index("rows") >> level) & 1 == 1


def edge_lanes(part):
    return lax.broadcasted_iota(jnp.int32, (RHS, LANES), 1) >> 5 == part


def head_kernel(vectors_hbm, weights_hbm, *refs):
    outputs, scratch = refs[: 2 * CHAINS + 1], refs[2 * CHAINS + 1 :]
    halves_ref = outputs[2 * CHAINS]
    vectors_ref, weights_ref, rows_ref, turned_ref, arranged_ref, sems = scratch
    copy = pltpu.make_async_copy(vectors_hbm, vectors_ref, sems.at[0])
    copy.start()
    pieces = []
    for piece in range(PIECES):
        size = RANK // PIECES
        for half in range(2):
            rows = pl.ds(half * RANK + piece * size, size)
            pieces.append(
                pltpu.make_async_copy(
                    weights_hbm.at[0, rows], weights_ref.at[rows], sems.at[1 + 2 * piece + half]
                )
            )
            pieces[-1].start()
    copy.wait()
    for half in range(2):
        lanes = slice(half * HALF, (half + 1) * HALF)
        for r in range(RHS):
            start = r * (RANK + 1)
            rows_ref[half, start : start + RANK, :] = vectors_ref[r, :, lanes].astype(F32)
        blocks = [rows_ref[half, pl.ds(a, RHS, stride=RANK + 1), :].astype(BF16) for a in range(RANK)]
        for q, block in enumerate(swap_major_lanes(blocks)):
            halves_ref[half, q] = block
    for piece in pieces:
        piece.wait()
    arrange_section(weights_ref, arranged_ref, turned_ref)
    upper = level_bit(0)
    for chain in range(CHAINS):
        own_ref, send_ref = outputs[2 * chain : 2 * chain + 2]
        for slot in range(SLOTS):
            q = chain * SLOTS + slot
            mixed = section_quad(arranged_ref, q, halves_ref[0, q], halves_ref[1, q]).astype(BF16)
            emit_halves(mixed, slot, upper, own_ref, send_ref)
        if chain == 0:
            edge = jnp.where(edge_lanes(0), halves_ref[0, 0], halves_ref[1, QUADS - 1])
            own_ref[SLOTS] = edge
            send_ref[SLOTS] = edge


def arrange_kernel(index, weights_ref, after_ref, arranged_ref, turned_ref):
    del after_ref
    arrange_section(weights_ref.at[index], arranged_ref, turned_ref)


def level_kernel(level, last, chain, *refs):
    arranged_ref, kept_ref, received_ref = refs[:3]
    outputs = refs[len(refs) - (3 if chain == 0 else 2) :]
    own_ref, send_ref = outputs[:2]
    upper = level_bit(level)
    next_upper = False if last else level_bit(level + 1)
    for slot in range(SLOTS):
        kept, received = kept_ref[slot], received_ref[slot]
        lower = jnp.where(upper, received, kept)
        higher = jnp.where(upper, kept, received)
        mixed = section_quad(arranged_ref, chain * SLOTS + slot, lower, higher).astype(BF16)
        emit_halves(mixed, slot, next_upper, own_ref, send_ref)
    if chain == 0:
        beside_ref, new_beside_ref = refs[3], outputs[2]
        inner = lax.axis_index("rows") & (2**level - 1)
        above = jnp.logical_and(jnp.logical_not(upper), inner == 2**level - 1)
        below = jnp.logical_and(upper, inner == 0)
        kept, received = kept_ref[SLOTS], received_ref[SLOTS]
        first, final = edge_lanes(0), edge_lanes(3)
        beside = jnp.where(jnp.logical_and(first, above), received, beside_ref[...])
        new_beside_ref[...] = jnp.where(jnp.logical_and(final, below), received, beside)
        if not last:
            theirs = jnp.logical_xor(first, jnp.logical_not(upper))
            edge = jnp.where(theirs, received, kept)
            own_ref[SLOTS] = edge
            send_ref[SLOTS] = edge


def near_kernel(halves_ref, blocks_ref, after_ref, near_ref, border_ref, arranged_ref, turned_ref):
    del after_ref
    first_group, last_group = edge_lanes(0), edge_lanes(3)
    zeros = jnp.zeros((RHS, LANES), BF16)
    for half in range(2):
        lanes = slice(half * HALF, (half + 1) * HALF)
        for a in range(RANK):
            shifts = [blocks_ref[shift, a, :, lanes] for shift in (0, 1, 2, 0)]
            turned = jnp.concatenate(shifts, axis=0).T.astype(F32)
            turned_ref[a * PITCH : a * PITCH + LANES, :] = turned
        for q in range(QUADS):
            rows = [turned_ref[pl.ds(part * QUADS + q, RANK, stride=PITCH), :] for part in range(4)]
            arranged_ref[q] = jnp.concatenate(rows, axis=0).astype(BF16).T
        if half == 0:
            border_ref[0] = arranged_ref[0, RANK : 2 * RANK, :]
        else:
            border_ref[1] = arranged_ref[QUADS - 1, 2 * RANK : 3 * RANK, :]
        edge_before = zeros if half == 0 else halves_ref[0, QUADS - 1]
        edge_after = zeros if half == 1 else halves_ref[1, 0]
        for q in range(QUADS):
            centre = halves_ref[half, q]
            if q > 0:
                before = halves_ref[half, q - 1]
            else:
                final = halves_ref[half, QUADS - 1]
                before = pltpu.roll(jnp.where(last_group, edge_before, final), RANK, 1)
            if q < QUADS - 1:
                after = halves_ref[half, q + 1]
            else:
                first = halves_ref[half, 0]
                after = pltpu.roll(jnp.where(first_group, edge_after, first), LANES - RANK, 1)
            tiles = [
                diagonal_blocks(arranged_ref[q, shift * RANK : (shift + 1) * RANK, :], part)
                for shift in range(3)
                for part in range(4)
            ]
            matrix = jnp.concatenate(tiles, axis=0)
            stack = jnp.concatenate([centre, before, after], axis=1)
            near_ref[half, q] = jnp.dot(stack, matrix, preferred_element_type=F32)


def border_term(border_ref, beside_ref, half):
    zeros = jnp.zeros((RHS, LANES), BF16)
    if half == 0:
        edge = pltpu.roll(jnp.where(edge_lanes(3), beside_ref[...], zeros), RANK, 1)
    else:
        edge = pltpu.roll(jnp.where(edge_lanes(0), beside_ref[...], zeros), LANES - RANK, 1)
    tiles = [diagonal_blocks(border_ref[half], part) for part in range(4)]
    return jnp.dot(edge, jnp.concatenate(tiles, axis=0), preferred_element_type=F32)


def root_kernel(*refs):
    arranged_ref, near_ref, border_ref, beside_ref = refs[:4]
    stacks, (product_ref, rows_ref) = refs[4 : 4 + 2 * CHAINS], refs[4 + 2 * CHAINS :]
    blocks = [[], []]
    for q in range(QUADS):
        chain, slot = divmod(q, SLOTS)
        mixed = section_quad(arranged_ref, q, stacks[2 * chain][slot], stacks[2 * chain + 1][slot])
        for half in range(2):
            total = mixed[:, half * LANES : (half + 1) * LANES] + near_ref[half, q]
            if q == half * (QUADS - 1):
                total = total + border_term(border_ref, beside_ref, half)
            blocks[half].append(total.astype(BF16))
    for half in range(2):
        lanes = slice(half * HALF, (half + 1) * HALF)
        for a, block in enumerate(swap_major_lanes(blocks[half])):
            start = a * (RHS + 1)
            rows_ref[half, start : start + RHS, :] = block.astype(F32)
        for r in range(RHS):
            product_ref[r, :, lanes] = rows_ref[half, pl.ds(r, RANK, stride=RHS + 1), :].astype(BF16)


VMEM_SPEC = pl.BlockSpec(memory_space=pltpu.VMEM)
ANY_SPEC = pl.BlockSpec(memory_space=pl.ANY)
HBM_SPEC = pl.BlockSpec(memory_space=pltpu.HBM)
TURNED = pltpu.VMEM((RANK * PITCH, LANES), F32)
ARRANGED = (QUADS, 2, 2 * RANK, LANES)
EDGE = jax.ShapeDtypeStruct((RHS, LANES), BF16)


def payload(chain, edge=True):
    return jax.ShapeDtypeStruct((SLOTS + (edge and chain == 0), RHS, LANES), BF16)


def params(mib):
    return pltpu.CompilerParams(vmem_limit_bytes=mib * 2**20)


def in_hbm(array):
    return pltpu.with_memory_space_constraint(array, pltpu.HBM)


def arrange(factors, index, after):
    return pl.pallas_call(
        functools.partial(arrange_kernel, index),
        out_shape=jax.ShapeDtypeStruct(ARRANGED, BF16),
        in_specs=[VMEM_SPEC, ANY_SPEC],
        out_specs=VMEM_SPEC,
        scratch_shapes=[TURNED],
        compiler_params=params(16),
        cost_estimate=pl.CostEstimate(flops=2 * 10**6, bytes_accessed=2 * 2**20, transcendentals=0),
        name="arrange",
    )(factors, after)


def head(vectors, factors):
    outs = [payload(chain) for chain in range(CHAINS) for _ in range(2)]
    *pairs, halves = pl.pallas_call(
        head_kernel,
        out_shape=(*outs, jax.ShapeDtypeStruct((2, QUADS, RHS, LANES), BF16)),
        in_specs=[HBM_SPEC, HBM_SPEC],
        out_specs=(VMEM_SPEC,) * (2 * CHAINS + 1),
        scratch_shapes=[
            pltpu.VMEM((RHS, RANK, 2 * HALF), BF16),
            pltpu.VMEM((2 * RANK, 2 * RANK, HALF), BF16),
            pltpu.VMEM((2, RHS * (RANK + 1), LANES), F32),
            TURNED,
            pltpu.VMEM(ARRANGED, BF16),
            pltpu.SemaphoreType.DMA((1 + 2 * PIECES,)),
        ],
        compiler_params=params(14),
        name="head",
    )(in_hbm(vectors), in_hbm(factors))
    return pairs[::2], pairs[1::2], halves


def level_step(level, last, chain, arranged, kept, received, beside, after=()):
    edges = [beside] if chain == 0 else []
    outs = [payload(chain, not last)] * 2 + [EDGE] * len(edges)
    return pl.pallas_call(
        functools.partial(level_kernel, level, last, chain),
        out_shape=tuple(outs),
        in_specs=[VMEM_SPEC] * (3 + len(edges)) + [ANY_SPEC] * len(after),
        out_specs=(VMEM_SPEC,) * len(outs),
        compiler_params=params(6),
        name="level",
    )(arranged, kept, received, *edges, *after)


def near_field(halves, neighbor_blocks, after):
    return pl.pallas_call(
        near_kernel,
        out_shape=(
            jax.ShapeDtypeStruct((2, QUADS, RHS, LANES), F32),
            jax.ShapeDtypeStruct((2, RANK, LANES), BF16),
        ),
        in_specs=[VMEM_SPEC, VMEM_SPEC, ANY_SPEC],
        out_specs=(VMEM_SPEC, VMEM_SPEC),
        scratch_shapes=[pltpu.VMEM((QUADS, LANES, LANES), BF16), TURNED],
        compiler_params=params(12),
        cost_estimate=pl.CostEstimate(flops=4 * 10**6, bytes_accessed=3 * 2**20, transcendentals=0),
        name="near",
    )(halves, neighbor_blocks, after)


def root(arranged, near, border, beside, stacks):
    return pl.pallas_call(
        root_kernel,
        out_shape=jax.ShapeDtypeStruct((RHS, RANK, 2 * HALF), BF16),
        in_specs=[VMEM_SPEC] * (4 + len(stacks)),
        out_specs=VMEM_SPEC,
        scratch_shapes=[pltpu.VMEM((2, (RHS + 1) * RANK, LANES), F32)],
        compiler_params=params(12),
        name="root",
    )(arranged, near, border, beside, *stacks)


def shards(vectors, factors, neighbor_blocks):
    level_count = factors.shape[0] - 2
    count = lax.axis_size("rows")
    kept, sending, halves = head(vectors, factors)
    beside = jnp.zeros(EDGE.shape, EDGE.dtype)
    for level in range(level_count):
        last = level == level_count - 1
        partners = [(i, i ^ (1 << level)) for i in range(count)]
        received = [lax.ppermute(part, "rows", partners) for part in sending]
        arranged = arrange(factors, level + 1, sending[-1])
        extra = ()
        if level == NEAR_LEVEL:
            near, border = near_field(halves, neighbor_blocks, sending[-1])
            extra = (near,)
        if last:
            root_arranged = arrange(factors, level_count + 1, sending[-1])
            extra = (root_arranged,)
        for chain in range(CHAINS):
            outs = level_step(
                level, last, chain, arranged, kept[chain], received[chain], beside, extra * (chain == 0)
            )
            kept[chain], sending[chain] = outs[:2]
            if chain == 0:
                beside = outs[2]
    stacks = [stack for pair in zip(kept, sending) for stack in pair]
    return root(root_arranged, near, border, beside, stacks)


def solution(mesh):
    placed = (P(None, None, "rows"), P(None, None, None, "rows"), P(None, None, None, "rows"))
    return jax.shard_map(
        shards, mesh=mesh, in_specs=placed, out_specs=P(None, None, "rows"), check_vma=False
    )
```

```python
import functools

import jax
import jax.numpy as jnp
from jax import lax
from jax.experimental import pallas as pl
from jax.experimental.pallas import tpu as pltpu
from jax.sharding import PartitionSpec as P

RHS = 16
RANK = 32
HALF = 128
QUADS = 32
LANES = 128
PITCH = LANES + 1
CHAINS = 2
SLOTS = QUADS // CHAINS
BF16 = jnp.bfloat16
F32 = jnp.float32


def lane_bit(shape, step, dtype=jnp.int32):
    return (lax.broadcasted_iota(dtype, shape, len(shape) - 1) & step) != 0


def swap_lane_groups(blocks):
    blocks = list(blocks)
    for step in (2, 1):
        lanes = step * QUADS
        upper = lane_bit(blocks[0].shape, lanes)
        for low in range(4):
            if low & step:
                continue
            high = low + step
            first, second = blocks[low], blocks[high]
            blocks[low] = jnp.where(upper, pltpu.roll(second, lanes, 1), first)
            blocks[high] = jnp.where(upper, second, pltpu.roll(first, LANES - lanes, 1))
    return blocks


def arrange_section(weights_ref, arranged_ref, turned_ref):
    for a in range(RANK):
        both = jnp.concatenate([weights_ref[a], weights_ref[RANK + a]], axis=0)
        turned_ref[a * PITCH : a * PITCH + LANES, :] = both.T.astype(F32)
    for q in range(QUADS):
        rows = [turned_ref[pl.ds(part * QUADS + q, RANK, stride=PITCH), :] for part in range(4)]
        turned = jnp.concatenate(rows, axis=0).astype(BF16).T
        arranged_ref[q] = turned.reshape(2, 2 * RANK, LANES)


def diagonal_blocks(block, group):
    lane = lax.broadcasted_iota(jnp.int32, block.shape, 1)
    return jnp.where((lane >> 5) & 3 == group, block, jnp.zeros_like(block))


def section_quad(arranged_ref, q, lower, higher):
    tiles = []
    for half in range(2):
        rows = slice(half * RANK, (half + 1) * RANK)
        dense = jnp.concatenate([arranged_ref[q, 0, rows, :], arranged_ref[q, 1, rows, :]], axis=1)
        tiles += [diagonal_blocks(dense, group) for group in range(4)]
    matrix = jnp.concatenate(tiles, axis=0)
    stack = jnp.concatenate([lower, higher], axis=1)
    return jnp.dot(stack, matrix, preferred_element_type=F32)


def emit_halves(mixed, q, upper, own_ref, send_ref):
    first, second = mixed[:, :LANES], mixed[:, LANES:]
    own_ref[q] = jnp.where(upper, second, first)
    send_ref[q] = jnp.where(upper, first, second)


def level_bit(level):
    return (lax.axis_index("rows") >> level) & 1 == 1


def edge_lanes(part):
    return lax.broadcasted_iota(jnp.int32, (RHS, LANES), 1) >> 5 == part


def head_kernel(vectors_hbm, weights_hbm, *refs):
    outputs, scratch = refs[: 2 * CHAINS + 2], refs[2 * CHAINS + 2 :]
    halves_ref, next_ref = outputs[2 * CHAINS :]
    vectors_ref, weights_ref, rows_ref, turned_ref, arranged_ref, sems = scratch
    copies = [
        pltpu.make_async_copy(vectors_hbm, vectors_ref, sems.at[0]),
        pltpu.make_async_copy(weights_hbm.at[0], weights_ref, sems.at[1]),
        pltpu.make_async_copy(weights_hbm.at[1], next_ref, sems.at[2]),
    ]
    for copy in copies:
        copy.start()
    copies[0].wait()
    for half in range(2):
        lanes = slice(half * HALF, (half + 1) * HALF)
        for e in range(4):
            parts = [
                swap_lane_groups([vectors_ref[4 * d + e, rows : rows + 16, lanes] for d in range(4)])
                for rows in (0, 16)
            ]
            tall = jnp.concatenate([parts[upper][g4] for g4 in range(4) for upper in range(2)], axis=0)
            turned = tall.T.astype(F32)
            for d in range(4):
                start = (4 * d + e) * (QUADS + 1)
                rows_ref[half, start : start + QUADS, :] = turned[d * QUADS : (d + 1) * QUADS, :]
        for q in range(QUADS):
            halves_ref[half, q] = rows_ref[half, pl.ds(q, RHS, stride=QUADS + 1), :].astype(BF16)
    copies[1].wait()
    arrange_section(weights_ref, arranged_ref, turned_ref)
    upper = level_bit(0)
    for chain in range(CHAINS):
        own_ref, send_ref = outputs[2 * chain : 2 * chain + 2]
        for slot in range(SLOTS):
            q = chain * SLOTS + slot
            mixed = section_quad(arranged_ref, q, halves_ref[0, q], halves_ref[1, q]).astype(BF16)
            emit_halves(mixed, slot, upper, own_ref, send_ref)
        if chain == 0:
            edge = jnp.where(edge_lanes(0), halves_ref[0, 0], halves_ref[1, QUADS - 1])
            own_ref[SLOTS] = edge
            send_ref[SLOTS] = edge
    copies[2].wait()


def arrange_kernel(index, weights_ref, after_ref, arranged_ref, turned_ref):
    del after_ref
    arrange_section(weights_ref if index is None else weights_ref.at[index], arranged_ref, turned_ref)


def mix_quad(arranged_ref, q, upper, kept, received):
    lower = jnp.where(upper, received, kept)
    higher = jnp.where(upper, kept, received)
    return section_quad(arranged_ref, q, lower, higher).astype(BF16)


def meet_border(level, upper, kept, received, beside):
    inner = lax.axis_index("rows") & (2**level - 1)
    above = jnp.logical_and(jnp.logical_not(upper), inner == 2**level - 1)
    below = jnp.logical_and(upper, inner == 0)
    beside = jnp.where(jnp.logical_and(edge_lanes(0), above), received, beside)
    return jnp.where(jnp.logical_and(edge_lanes(3), below), received, beside)


def level_kernel(level, chain, merge, *refs):
    arranged_ref, kept_ref, received_ref = refs[:3]
    outputs = refs[len(refs) - (3 if chain == 0 else 2) :]
    own_ref, send_ref = outputs[:2]
    upper, next_upper = level_bit(level), level_bit(level + 1)
    for slot in range(SLOTS):
        q = chain * SLOTS + slot
        mixed = mix_quad(arranged_ref, q, upper, kept_ref[slot], received_ref[slot])
        emit_halves(mixed, q if merge else slot, next_upper, own_ref, send_ref)
    if chain == 0:
        kept, received = kept_ref[SLOTS], received_ref[SLOTS]
        outputs[2][...] = meet_border(level, upper, kept, received, refs[3][...])
        theirs = jnp.logical_xor(edge_lanes(0), jnp.logical_not(upper))
        edge = jnp.where(theirs, received, kept)
        place = QUADS if merge else SLOTS
        own_ref[place] = edge
        send_ref[place] = edge


def near_kernel(halves_ref, blocks_ref, after_ref, near_ref, border_ref, arranged_ref, turned_ref):
    del after_ref
    first_group, last_group = edge_lanes(0), edge_lanes(3)
    zeros = jnp.zeros((RHS, LANES), BF16)
    for half in range(2):
        lanes = slice(half * HALF, (half + 1) * HALF)
        for a in range(RANK):
            shifts = [blocks_ref[shift, a, :, lanes] for shift in (0, 1, 2, 0)]
            turned = jnp.concatenate(shifts, axis=0).T.astype(F32)
            turned_ref[a * PITCH : a * PITCH + LANES, :] = turned
        for q in range(QUADS):
            rows = [turned_ref[pl.ds(part * QUADS + q, RANK, stride=PITCH), :] for part in range(4)]
            arranged_ref[q] = jnp.concatenate(rows, axis=0).astype(BF16).T
        if half == 0:
            border_ref[0] = arranged_ref[0, RANK : 2 * RANK, :]
        else:
            border_ref[1] = arranged_ref[QUADS - 1, 2 * RANK : 3 * RANK, :]
        edge_before = zeros if half == 0 else halves_ref[0, QUADS - 1]
        edge_after = zeros if half == 1 else halves_ref[1, 0]
        for q in range(QUADS):
            centre = halves_ref[half, q]
            if q > 0:
                before = halves_ref[half, q - 1]
            else:
                final = halves_ref[half, QUADS - 1]
                before = pltpu.roll(jnp.where(last_group, edge_before, final), RANK, 1)
            if q < QUADS - 1:
                after = halves_ref[half, q + 1]
            else:
                first = halves_ref[half, 0]
                after = pltpu.roll(jnp.where(first_group, edge_after, first), LANES - RANK, 1)
            tiles = [
                diagonal_blocks(arranged_ref[q, shift * RANK : (shift + 1) * RANK, :], part)
                for shift in range(3)
                for part in range(4)
            ]
            matrix = jnp.concatenate(tiles, axis=0)
            stack = jnp.concatenate([centre, before, after], axis=1)
            near_ref[half, q] = jnp.dot(stack, matrix, preferred_element_type=F32)


def border_term(border_ref, beside, half):
    zeros = jnp.zeros((RHS, LANES), BF16)
    if half == 0:
        edge = pltpu.roll(jnp.where(edge_lanes(3), beside, zeros), RANK, 1)
    else:
        edge = pltpu.roll(jnp.where(edge_lanes(0), beside, zeros), LANES - RANK, 1)
    tiles = [diagonal_blocks(border_ref[half], part) for part in range(4)]
    return jnp.dot(edge, jnp.concatenate(tiles, axis=0), preferred_element_type=F32)


def tail_kernel(
    level, last_ref, root_ref, kept_ref, received_ref, beside_ref, near_ref, border_ref, product_ref, rows_ref
):
    upper = level_bit(level)
    beside = meet_border(level, upper, kept_ref[QUADS], received_ref[QUADS], beside_ref[...])
    for q in range(QUADS):
        mixed = mix_quad(last_ref, q, upper, kept_ref[q], received_ref[q])
        mixed = section_quad(root_ref, q, mixed[:, :LANES], mixed[:, LANES:])
        for half in range(2):
            total = mixed[:, half * LANES : (half + 1) * LANES] + near_ref[half, q]
            if q == half * (QUADS - 1):
                total = total + border_term(border_ref, beside, half)
            rows_ref[half, q * (RHS + 1) : q * (RHS + 1) + RHS, :] = total
    for half in range(2):
        lanes = slice(half * HALF, (half + 1) * HALF)
        for e in range(4):
            rows = [rows_ref[half, pl.ds(4 * d + e, QUADS, stride=RHS + 1), :] for d in range(4)]
            turned = jnp.concatenate(rows, axis=0).astype(BF16).T
            for row in (0, 16):
                blocks = [turned[g4 * RANK + row : g4 * RANK + row + 16, :] for g4 in range(4)]
                for d, block in enumerate(swap_lane_groups(blocks)):
                    product_ref[4 * d + e, row : row + 16, lanes] = block


VMEM_SPEC = pl.BlockSpec(memory_space=pltpu.VMEM)
ANY_SPEC = pl.BlockSpec(memory_space=pl.ANY)
HBM_SPEC = pl.BlockSpec(memory_space=pltpu.HBM)
TURNED = pltpu.VMEM((RANK * PITCH, LANES), F32)
ARRANGED = (QUADS, 2, 2 * RANK, LANES)
EDGE = jax.ShapeDtypeStruct((RHS, LANES), BF16)


def payload(chain, merge=False):
    slots = QUADS + 1 if merge else SLOTS + (chain == 0)
    return jax.ShapeDtypeStruct((slots, RHS, LANES), BF16)


def params(mib):
    return pltpu.CompilerParams(vmem_limit_bytes=mib * 2**20)


def in_hbm(array):
    return pltpu.with_memory_space_constraint(array, pltpu.HBM)


def arrange(factors, index, after):
    return pl.pallas_call(
        functools.partial(arrange_kernel, index),
        out_shape=jax.ShapeDtypeStruct(ARRANGED, BF16),
        in_specs=[VMEM_SPEC, ANY_SPEC],
        out_specs=VMEM_SPEC,
        scratch_shapes=[TURNED],
        compiler_params=params(16),
        cost_estimate=pl.CostEstimate(flops=2 * 10**6, bytes_accessed=2 * 2**20, transcendentals=0),
        name="arrange",
    )(factors, after)


def head(vectors, factors):
    section = (2 * RANK, 2 * RANK, HALF)
    outs = [payload(chain) for chain in range(CHAINS) for _ in range(2)]
    outs += [jax.ShapeDtypeStruct((2, QUADS, RHS, LANES), BF16), jax.ShapeDtypeStruct(section, BF16)]
    *pairs, halves, section_1 = pl.pallas_call(
        head_kernel,
        out_shape=tuple(outs),
        in_specs=[HBM_SPEC, HBM_SPEC],
        out_specs=(VMEM_SPEC,) * len(outs),
        scratch_shapes=[
            pltpu.VMEM((RHS, RANK, 2 * HALF), BF16),
            pltpu.VMEM(section, BF16),
            pltpu.VMEM((2, RHS * (QUADS + 1), LANES), F32),
            TURNED,
            pltpu.VMEM(ARRANGED, BF16),
            pltpu.SemaphoreType.DMA((3,)),
        ],
        compiler_params=params(14),
        name="head",
    )(in_hbm(vectors), in_hbm(factors))
    return pairs[::2], pairs[1::2], halves, section_1


def level_step(level, chain, arranged, kept, received, beside, into=None):
    merge = into is not None
    edges = [beside] if chain == 0 else []
    filled = list(into) if merge and chain > 0 else []
    outs = [payload(chain, merge)] * 2 + [EDGE] * len(edges)
    return pl.pallas_call(
        functools.partial(level_kernel, level, chain, merge),
        out_shape=tuple(outs),
        in_specs=[VMEM_SPEC] * (3 + len(edges) + len(filled)),
        out_specs=(VMEM_SPEC,) * len(outs),
        input_output_aliases={3: 0, 4: 1} if filled else {},
        compiler_params=params(6),
        name="level",
    )(arranged, kept, received, *edges, *filled)


def near_field(halves, neighbor_blocks, after):
    return pl.pallas_call(
        near_kernel,
        out_shape=(
            jax.ShapeDtypeStruct((2, QUADS, RHS, LANES), F32),
            jax.ShapeDtypeStruct((2, RANK, LANES), BF16),
        ),
        in_specs=[VMEM_SPEC, VMEM_SPEC, ANY_SPEC],
        out_specs=(VMEM_SPEC, VMEM_SPEC),
        scratch_shapes=[pltpu.VMEM((QUADS, LANES, LANES), BF16), TURNED],
        compiler_params=params(12),
        cost_estimate=pl.CostEstimate(flops=4 * 10**6, bytes_accessed=3 * 2**20, transcendentals=0),
        name="near",
    )(halves, neighbor_blocks, after)


def tail(level, *operands):
    return pl.pallas_call(
        functools.partial(tail_kernel, level),
        out_shape=jax.ShapeDtypeStruct((RHS, RANK, 2 * HALF), BF16),
        in_specs=[VMEM_SPEC] * len(operands),
        out_specs=VMEM_SPEC,
        scratch_shapes=[pltpu.VMEM((2, QUADS * (RHS + 1), LANES), F32)],
        compiler_params=params(12),
        name="tail",
    )(*operands)


def shards(vectors, factors, neighbor_blocks):
    level_count = factors.shape[0] - 2
    count = lax.axis_size("rows")
    kept, sending, halves, section_1 = head(vectors, factors)
    sending[0], factors = lax.optimization_barrier((sending[0], factors))
    beside = jnp.zeros(EDGE.shape, EDGE.dtype)
    for level in range(level_count - 1):
        partners = [(i, i ^ (1 << level)) for i in range(count)]
        received = [lax.ppermute(part, "rows", partners) for part in sending]
        if level == 0:
            arranged = arrange(section_1, None, sending[-1])
        else:
            arranged = arrange(factors, level + 1, sending[-1])
        into = () if level == level_count - 2 else None
        for chain in range(CHAINS):
            outs = level_step(level, chain, arranged, kept[chain], received[chain], beside, into)
            kept[chain], sending[chain] = outs[:2]
            if chain == 0:
                beside = outs[2]
            if into is not None:
                into = outs[:2]
    level = level_count - 1
    kept, sending = into
    received = lax.ppermute(sending, "rows", [(i, i ^ (1 << level)) for i in range(count)])
    near, border = near_field(halves, neighbor_blocks, sending)
    last = arrange(factors, level + 1, sending)
    root = arrange(factors, level + 2, sending)
    return tail(level, last, root, kept, received, beside, near, border)


def solution(mesh):
    placed = (P(None, None, "rows"), P(None, None, None, "rows"), P(None, None, None, "rows"))
    return jax.shard_map(
        shards, mesh=mesh, in_specs=placed, out_specs=P(None, None, "rows"), check_vma=False
    )
```

```python
import functools

import jax
import jax.numpy as jnp
from jax import lax
from jax.experimental import pallas as pl
from jax.experimental.pallas import tpu as pltpu
from jax.sharding import PartitionSpec as P

RHS = 16
RANK = 32
HALF = 128
QUADS = 32
LANES = 128
PITCH = LANES + 1
CHAINS = 2
SLOTS = QUADS // CHAINS
BF16 = jnp.bfloat16
F32 = jnp.float32


def lane_bit(shape, step, dtype=jnp.int32):
    return (lax.broadcasted_iota(dtype, shape, len(shape) - 1) & step) != 0


def swap_lane_groups(blocks):
    blocks = list(blocks)
    for step in (2, 1):
        lanes = step * QUADS
        upper = lane_bit(blocks[0].shape, lanes)
        for low in range(4):
            if low & step:
                continue
            high = low + step
            first, second = blocks[low], blocks[high]
            blocks[low] = jnp.where(upper, pltpu.roll(second, lanes, 1), first)
            blocks[high] = jnp.where(upper, second, pltpu.roll(first, LANES - lanes, 1))
    return blocks


def turn_section(weights_ref, turned_ref):
    for a in range(RANK):
        both = jnp.concatenate([weights_ref[a], weights_ref[RANK + a]], axis=0)
        turned_ref[a * PITCH : a * PITCH + LANES, :] = both.T.astype(F32)


def dense_quad(turned_ref, q):
    rows = [turned_ref[pl.ds(part * QUADS + q, RANK, stride=PITCH), :] for part in range(4)]
    return jnp.concatenate(rows, axis=0).astype(BF16).T


def arrange_section(weights_ref, arranged_ref, turned_ref):
    turn_section(weights_ref, turned_ref)
    for q in range(QUADS):
        arranged_ref[q] = dense_quad(turned_ref, q).reshape(2, 2 * RANK, LANES)


def diagonal_blocks(block, group):
    lane = lax.broadcasted_iota(jnp.int32, block.shape, 1)
    return jnp.where((lane >> 5) & 3 == group, block, jnp.zeros_like(block))


def section_quad(arranged_ref, q, lower, higher):
    tiles = []
    for half in range(2):
        rows = slice(half * RANK, (half + 1) * RANK)
        dense = jnp.concatenate([arranged_ref[q, 0, rows, :], arranged_ref[q, 1, rows, :]], axis=1)
        tiles += [diagonal_blocks(dense, group) for group in range(4)]
    matrix = jnp.concatenate(tiles, axis=0)
    stack = jnp.concatenate([lower, higher], axis=1)
    return jnp.dot(stack, matrix, preferred_element_type=F32)


def half_dot(stack, pair):
    dense = jnp.concatenate(pair, axis=1)
    matrix = jnp.concatenate([diagonal_blocks(dense, group) for group in range(4)], axis=0)
    return jnp.dot(stack, matrix, preferred_element_type=F32)


def emit_halves(mixed, q, upper, own_ref, send_ref):
    first, second = mixed[:, :LANES], mixed[:, LANES:]
    own_ref[q] = jnp.where(upper, second, first)
    send_ref[q] = jnp.where(upper, first, second)


def level_bit(level):
    return (lax.axis_index("rows") >> level) & 1 == 1


def edge_lanes(part):
    return lax.broadcasted_iota(jnp.int32, (RHS, LANES), 1) >> 5 == part


def head_kernel(vectors_hbm, weights_hbm, *refs):
    outputs, scratch = refs[: 2 * CHAINS + 2], refs[2 * CHAINS + 2 :]
    halves_ref, next_ref = outputs[2 * CHAINS :]
    vectors_ref, weights_ref, rows_ref, turned_ref, arranged_ref, sems = scratch
    copies = [
        pltpu.make_async_copy(
            vectors_hbm.at[:, :, pl.ds(half * HALF, HALF)], vectors_ref.at[half], sems.at[half]
        )
        for half in range(2)
    ]
    copies += [
        pltpu.make_async_copy(weights_hbm.at[0], weights_ref, sems.at[2]),
        pltpu.make_async_copy(weights_hbm.at[1], next_ref, sems.at[3]),
    ]
    for copy in copies:
        copy.start()
    for half in range(2):
        copies[half].wait()
        for e in range(4):
            parts = [
                swap_lane_groups([vectors_ref[half, 4 * d + e, rows : rows + 16, :] for d in range(4)])
                for rows in (0, 16)
            ]
            tall = jnp.concatenate([parts[upper][g4] for g4 in range(4) for upper in range(2)], axis=0)
            turned = tall.T.astype(F32)
            for d in range(4):
                start = (4 * d + e) * (QUADS + 1)
                rows_ref[half, start : start + QUADS, :] = turned[d * QUADS : (d + 1) * QUADS, :]
        for q in range(QUADS):
            halves_ref[half, q] = rows_ref[half, pl.ds(q, RHS, stride=QUADS + 1), :].astype(BF16)
    copies[2].wait()
    arrange_section(weights_ref, arranged_ref, turned_ref)
    upper = level_bit(0)
    for chain in range(CHAINS):
        own_ref, send_ref = outputs[2 * chain : 2 * chain + 2]
        for slot in range(SLOTS):
            q = chain * SLOTS + slot
            mixed = section_quad(arranged_ref, q, halves_ref[0, q], halves_ref[1, q]).astype(BF16)
            emit_halves(mixed, slot, upper, own_ref, send_ref)
        if chain == 0:
            edge = jnp.where(edge_lanes(0), halves_ref[0, 0], halves_ref[1, QUADS - 1])
            own_ref[SLOTS] = edge
            send_ref[SLOTS] = edge
    copies[3].wait()


def arrange_kernel(index, weights_ref, after_ref, arranged_ref, turned_ref):
    del after_ref
    arrange_section(weights_ref.at[index], arranged_ref, turned_ref)


def stage_kernel(level, index, chains, *refs):
    weights_ref, *kept_refs = refs[: 1 + chains]
    partial_ref, arranged_ref, turned_ref = refs[len(refs) - 3 :]
    upper = level_bit(level)
    turn_section(weights_ref if index is None else weights_ref.at[index], turned_ref)
    for q in range(QUADS):
        dense = dense_quad(turned_ref, q)
        low, high = [
            [dense[(2 * k + half) * RANK : (2 * k + half + 1) * RANK] for k in range(2)] for half in range(2)
        ]
        mine = [jnp.where(upper, second, first) for first, second in zip(low, high)]
        chain, slot = divmod(q, QUADS // chains)
        partial_ref[q] = half_dot(kept_refs[chain][slot], mine)
        for k in range(2):
            arranged_ref[q, k] = jnp.where(upper, low[k], high[k])


def arrive(partial_ref, arranged_ref, q, received):
    mixed = half_dot(received, [arranged_ref[q, 0], arranged_ref[q, 1]])
    return (mixed + partial_ref[q]).astype(BF16)


def meet_border(level, upper, kept, received, beside):
    inner = lax.axis_index("rows") & (2**level - 1)
    above = jnp.logical_and(jnp.logical_not(upper), inner == 2**level - 1)
    below = jnp.logical_and(upper, inner == 0)
    beside = jnp.where(jnp.logical_and(edge_lanes(0), above), received, beside)
    return jnp.where(jnp.logical_and(edge_lanes(3), below), received, beside)


def level_kernel(level, chain, merge, *refs):
    partial_ref, arranged_ref, received_ref = refs[:3]
    outputs = refs[len(refs) - (3 if chain == 0 else 2) :]
    own_ref, send_ref = outputs[:2]
    upper, next_upper = level_bit(level), level_bit(level + 1)
    for slot in range(SLOTS):
        q = chain * SLOTS + slot
        mixed = arrive(partial_ref, arranged_ref, q, received_ref[slot])
        emit_halves(mixed, q if merge else slot, next_upper, own_ref, send_ref)
    if chain == 0:
        kept, received = refs[3][SLOTS], received_ref[SLOTS]
        outputs[2][...] = meet_border(level, upper, kept, received, refs[4][...])
        theirs = jnp.logical_xor(edge_lanes(0), jnp.logical_not(upper))
        edge = jnp.where(theirs, received, kept)
        place = QUADS if merge else SLOTS
        own_ref[place] = edge
        send_ref[place] = edge


def near_kernel(halves_ref, blocks_ref, after_ref, near_ref, border_ref, arranged_ref, turned_ref):
    del after_ref
    first_group, last_group = edge_lanes(0), edge_lanes(3)
    zeros = jnp.zeros((RHS, LANES), BF16)
    for half in range(2):
        lanes = slice(half * HALF, (half + 1) * HALF)
        for a in range(RANK):
            shifts = [blocks_ref[shift, a, :, lanes] for shift in (0, 1, 2, 0)]
            turned = jnp.concatenate(shifts, axis=0).T.astype(F32)
            turned_ref[a * PITCH : a * PITCH + LANES, :] = turned
        for q in range(QUADS):
            arranged_ref[q] = dense_quad(turned_ref, q)
        if half == 0:
            border_ref[0] = arranged_ref[0, RANK : 2 * RANK, :]
        else:
            border_ref[1] = arranged_ref[QUADS - 1, 2 * RANK : 3 * RANK, :]
        edge_before = zeros if half == 0 else halves_ref[0, QUADS - 1]
        edge_after = zeros if half == 1 else halves_ref[1, 0]
        for q in range(QUADS):
            centre = halves_ref[half, q]
            if q > 0:
                before = halves_ref[half, q - 1]
            else:
                final = halves_ref[half, QUADS - 1]
                before = pltpu.roll(jnp.where(last_group, edge_before, final), RANK, 1)
            if q < QUADS - 1:
                after = halves_ref[half, q + 1]
            else:
                first = halves_ref[half, 0]
                after = pltpu.roll(jnp.where(first_group, edge_after, first), LANES - RANK, 1)
            tiles = [
                diagonal_blocks(arranged_ref[q, shift * RANK : (shift + 1) * RANK, :], part)
                for shift in range(3)
                for part in range(4)
            ]
            matrix = jnp.concatenate(tiles, axis=0)
            stack = jnp.concatenate([centre, before, after], axis=1)
            near_ref[half, q] = jnp.dot(stack, matrix, preferred_element_type=F32)


def border_term(border_ref, beside, half):
    zeros = jnp.zeros((RHS, LANES), BF16)
    if half == 0:
        edge = pltpu.roll(jnp.where(edge_lanes(3), beside, zeros), RANK, 1)
    else:
        edge = pltpu.roll(jnp.where(edge_lanes(0), beside, zeros), LANES - RANK, 1)
    tiles = [diagonal_blocks(border_ref[half], part) for part in range(4)]
    return jnp.dot(edge, jnp.concatenate(tiles, axis=0), preferred_element_type=F32)


def tail_kernel(
    level,
    partial_ref,
    last_ref,
    root_ref,
    kept_ref,
    received_ref,
    beside_ref,
    near_ref,
    border_ref,
    product_ref,
    coeffs_ref,
    rows_ref,
):
    for q in range(QUADS):
        coeffs_ref[q] = arrive(partial_ref, last_ref, q, received_ref[q])
    beside = meet_border(level, level_bit(level), kept_ref[QUADS], received_ref[QUADS], beside_ref[...])
    for q in range(QUADS):
        mixed = section_quad(root_ref, q, coeffs_ref[q, :, :LANES], coeffs_ref[q, :, LANES:])
        for half in range(2):
            total = mixed[:, half * LANES : (half + 1) * LANES] + near_ref[half, q]
            if q == half * (QUADS - 1):
                total = total + border_term(border_ref, beside, half)
            rows_ref[half, q * (RHS + 1) : q * (RHS + 1) + RHS, :] = total
    for half in range(2):
        lanes = slice(half * HALF, (half + 1) * HALF)
        for e in range(4):
            rows = [rows_ref[half, pl.ds(4 * d + e, QUADS, stride=RHS + 1), :] for d in range(4)]
            turned = jnp.concatenate(rows, axis=0).astype(BF16).T
            for row in (0, 16):
                blocks = [turned[g4 * RANK + row : g4 * RANK + row + 16, :] for g4 in range(4)]
                for d, block in enumerate(swap_lane_groups(blocks)):
                    product_ref[4 * d + e, row : row + 16, lanes] = block


VMEM_SPEC = pl.BlockSpec(memory_space=pltpu.VMEM)
ANY_SPEC = pl.BlockSpec(memory_space=pl.ANY)
HBM_SPEC = pl.BlockSpec(memory_space=pltpu.HBM)
TURNED = pltpu.VMEM((RANK * PITCH, LANES), F32)
ARRANGED = (QUADS, 2, 2 * RANK, LANES)
EDGE = jax.ShapeDtypeStruct((RHS, LANES), BF16)


def payload(chain, merge=False):
    slots = QUADS + 1 if merge else SLOTS + (chain == 0)
    return jax.ShapeDtypeStruct((slots, RHS, LANES), BF16)


def params(mib):
    return pltpu.CompilerParams(vmem_limit_bytes=mib * 2**20)


def in_hbm(array):
    return pltpu.with_memory_space_constraint(array, pltpu.HBM)


def arrange(factors, index, after):
    return pl.pallas_call(
        functools.partial(arrange_kernel, index),
        out_shape=jax.ShapeDtypeStruct(ARRANGED, BF16),
        in_specs=[VMEM_SPEC, ANY_SPEC],
        out_specs=VMEM_SPEC,
        scratch_shapes=[TURNED],
        compiler_params=params(16),
        cost_estimate=pl.CostEstimate(flops=2 * 10**6, bytes_accessed=2 * 2**20, transcendentals=0),
        name="arrange",
    )(factors, after)


def stage(level, weights, index, kept, after):
    return pl.pallas_call(
        functools.partial(stage_kernel, level, index, len(kept)),
        out_shape=(
            jax.ShapeDtypeStruct((QUADS, RHS, 2 * LANES), F32),
            jax.ShapeDtypeStruct((QUADS, 2, RANK, LANES), BF16),
        ),
        in_specs=[VMEM_SPEC] * (1 + len(kept)) + [ANY_SPEC],
        out_specs=(VMEM_SPEC, VMEM_SPEC),
        scratch_shapes=[TURNED],
        compiler_params=params(16),
        cost_estimate=pl.CostEstimate(flops=2 * 10**6, bytes_accessed=2 * 2**20, transcendentals=0),
        name="stage",
    )(weights, *kept, after)


def head(vectors, factors):
    section = (2 * RANK, 2 * RANK, HALF)
    outs = [payload(chain) for chain in range(CHAINS) for _ in range(2)]
    outs += [jax.ShapeDtypeStruct((2, QUADS, RHS, LANES), BF16), jax.ShapeDtypeStruct(section, BF16)]
    *pairs, halves, section_1 = pl.pallas_call(
        head_kernel,
        out_shape=tuple(outs),
        in_specs=[HBM_SPEC, HBM_SPEC],
        out_specs=(VMEM_SPEC,) * len(outs),
        scratch_shapes=[
            pltpu.VMEM((2, RHS, RANK, HALF), BF16),
            pltpu.VMEM(section, BF16),
            pltpu.VMEM((2, RHS * (QUADS + 1), LANES), F32),
            TURNED,
            pltpu.VMEM(ARRANGED, BF16),
            pltpu.SemaphoreType.DMA((4,)),
        ],
        compiler_params=params(14),
        name="head",
    )(in_hbm(vectors), in_hbm(factors))
    return pairs[::2], pairs[1::2], halves, section_1


def level_step(level, chain, partial, arranged, kept, received, beside, into=None):
    merge = into is not None
    edges = [kept, beside] if chain == 0 else []
    filled = list(into) if merge and chain > 0 else []
    outs = [payload(chain, merge)] * 2 + [EDGE] * (chain == 0)
    return pl.pallas_call(
        functools.partial(level_kernel, level, chain, merge),
        out_shape=tuple(outs),
        in_specs=[VMEM_SPEC] * (3 + len(edges) + len(filled)),
        out_specs=(VMEM_SPEC,) * len(outs),
        input_output_aliases={3: 0, 4: 1} if filled else {},
        compiler_params=params(6),
        name="level",
    )(partial, arranged, received, *edges, *filled)


def near_field(halves, neighbor_blocks, after):
    return pl.pallas_call(
        near_kernel,
        out_shape=(
            jax.ShapeDtypeStruct((2, QUADS, RHS, LANES), F32),
            jax.ShapeDtypeStruct((2, RANK, LANES), BF16),
        ),
        in_specs=[VMEM_SPEC, VMEM_SPEC, ANY_SPEC],
        out_specs=(VMEM_SPEC, VMEM_SPEC),
        scratch_shapes=[pltpu.VMEM((QUADS, LANES, LANES), BF16), TURNED],
        compiler_params=params(12),
        cost_estimate=pl.CostEstimate(flops=4 * 10**6, bytes_accessed=3 * 2**20, transcendentals=0),
        name="near",
    )(halves, neighbor_blocks, after)


def tail(level, *operands):
    return pl.pallas_call(
        functools.partial(tail_kernel, level),
        out_shape=jax.ShapeDtypeStruct((RHS, RANK, 2 * HALF), BF16),
        in_specs=[VMEM_SPEC] * len(operands),
        out_specs=VMEM_SPEC,
        scratch_shapes=[
            pltpu.VMEM((QUADS, RHS, 2 * LANES), BF16),
            pltpu.VMEM((2, QUADS * (RHS + 1), LANES), F32),
        ],
        compiler_params=params(12),
        name="tail",
    )(*operands)


def shards(vectors, factors, neighbor_blocks):
    level_count = factors.shape[0] - 2
    count = lax.axis_size("rows")
    kept, sending, halves, section_1 = head(vectors, factors)
    sending[0], factors = lax.optimization_barrier((sending[0], factors))
    beside = jnp.zeros(EDGE.shape, EDGE.dtype)
    for level in range(level_count - 1):
        partners = [(i, i ^ (1 << level)) for i in range(count)]
        received = [lax.ppermute(part, "rows", partners) for part in sending]
        if level == 0:
            staged = stage(level, section_1, None, kept, sending[-1])
        else:
            staged = stage(level, factors, level + 1, kept, sending[-1])
        into = () if level == level_count - 2 else None
        for chain in range(CHAINS):
            outs = level_step(level, chain, *staged, kept[chain], received[chain], beside, into)
            kept[chain], sending[chain] = outs[:2]
            if chain == 0:
                beside = outs[2]
            if into is not None:
                into = outs[:2]
    level = level_count - 1
    kept, sending = into
    received = lax.ppermute(sending, "rows", [(i, i ^ (1 << level)) for i in range(count)])
    near, border = near_field(halves, neighbor_blocks, sending)
    partial, last = stage(level, factors, level + 1, [kept], sending)
    root = arrange(factors, level + 2, sending)
    return tail(level, partial, last, root, kept, received, beside, near, border)


def solution(mesh):
    placed = (P(None, None, "rows"), P(None, None, None, "rows"), P(None, None, None, "rows"))
    return jax.shard_map(
        shards, mesh=mesh, in_specs=placed, out_specs=P(None, None, "rows"), check_vma=False
    )
```

```python
import functools

import jax
import jax.numpy as jnp
from jax import lax
from jax.experimental import pallas as pl
from jax.experimental.pallas import tpu as pltpu
from jax.sharding import PartitionSpec as P

RHS = 16
RANK = 32
HALF = 128
QUADS = 32
LANES = 128
PITCH = LANES + 1
CHAINS = 2
SLOTS = QUADS // CHAINS
BF16 = jnp.bfloat16
F32 = jnp.float32


def lane_bit(shape, step, dtype=jnp.int32):
    return (lax.broadcasted_iota(dtype, shape, len(shape) - 1) & step) != 0


def swap_lane_groups(blocks):
    blocks = list(blocks)
    for step in (2, 1):
        lanes = step * QUADS
        upper = lane_bit(blocks[0].shape, lanes)
        for low in range(4):
            if low & step:
                continue
            high = low + step
            first, second = blocks[low], blocks[high]
            blocks[low] = jnp.where(upper, pltpu.roll(second, lanes, 1), first)
            blocks[high] = jnp.where(upper, second, pltpu.roll(first, LANES - lanes, 1))
    return blocks


def turn_section(weights_ref, turned_ref):
    for a in range(RANK):
        both = jnp.concatenate([weights_ref[a], weights_ref[RANK + a]], axis=0)
        turned_ref[a * PITCH : a * PITCH + LANES, :] = both.T.astype(F32)


def dense_quad(turned_ref, q):
    rows = [turned_ref[pl.ds(part * QUADS + q, RANK, stride=PITCH), :] for part in range(4)]
    return jnp.concatenate(rows, axis=0).astype(BF16).T


def arrange_section(weights_ref, arranged_ref, turned_ref):
    turn_section(weights_ref, turned_ref)
    for q in range(QUADS):
        arranged_ref[q] = dense_quad(turned_ref, q).reshape(2, 2 * RANK, LANES)


def diagonal_blocks(block, group):
    lane = lax.broadcasted_iota(jnp.int32, block.shape, 1)
    return jnp.where((lane >> 5) & 3 == group, block, jnp.zeros_like(block))


def section_quad(arranged_ref, q, lower, higher):
    tiles = []
    for half in range(2):
        rows = slice(half * RANK, (half + 1) * RANK)
        dense = jnp.concatenate([arranged_ref[q, 0, rows, :], arranged_ref[q, 1, rows, :]], axis=1)
        tiles += [diagonal_blocks(dense, group) for group in range(4)]
    matrix = jnp.concatenate(tiles, axis=0)
    stack = jnp.concatenate([lower, higher], axis=1)
    return jnp.dot(stack, matrix, preferred_element_type=F32)


def half_dot(stack, pair):
    dense = jnp.concatenate(pair, axis=1)
    matrix = jnp.concatenate([diagonal_blocks(dense, group) for group in range(4)], axis=0)
    return jnp.dot(stack, matrix, preferred_element_type=F32)


def emit_halves(mixed, q, upper, own_ref, send_ref):
    first, second = mixed[:, :LANES], mixed[:, LANES:]
    own_ref[q] = jnp.where(upper, second, first)
    send_ref[q] = jnp.where(upper, first, second)


def level_bit(level):
    return (lax.axis_index("rows") >> level) & 1 == 1


def edge_lanes(part):
    return lax.broadcasted_iota(jnp.int32, (RHS, LANES), 1) >> 5 == part


def head_kernel(vectors_hbm, weights_hbm, *refs):
    outputs, scratch = refs[: 2 * CHAINS + 2], refs[2 * CHAINS + 2 :]
    halves_ref, next_ref = outputs[2 * CHAINS :]
    vectors_ref, weights_ref, rows_ref, turned_ref, arranged_ref, sems = scratch
    copies = [
        pltpu.make_async_copy(
            vectors_hbm.at[:, :, pl.ds(half * HALF, HALF)], vectors_ref.at[half], sems.at[half]
        )
        for half in range(2)
    ]
    copies += [
        pltpu.make_async_copy(weights_hbm.at[0], weights_ref, sems.at[2]),
        pltpu.make_async_copy(weights_hbm.at[1], next_ref, sems.at[3]),
    ]
    for copy in copies:
        copy.start()
    for half in range(2):
        copies[half].wait()
        for e in range(4):
            parts = [
                swap_lane_groups([vectors_ref[half, 4 * d + e, rows : rows + 16, :] for d in range(4)])
                for rows in (0, 16)
            ]
            tall = jnp.concatenate([parts[upper][g4] for g4 in range(4) for upper in range(2)], axis=0)
            turned = tall.T.astype(F32)
            for d in range(4):
                start = (4 * d + e) * (QUADS + 1)
                rows_ref[half, start : start + QUADS, :] = turned[d * QUADS : (d + 1) * QUADS, :]
        for q in range(QUADS):
            halves_ref[half, q] = rows_ref[half, pl.ds(q, RHS, stride=QUADS + 1), :].astype(BF16)
    copies[2].wait()
    arrange_section(weights_ref, arranged_ref, turned_ref)
    upper = level_bit(0)
    for chain in range(CHAINS):
        own_ref, send_ref = outputs[2 * chain : 2 * chain + 2]
        for slot in range(SLOTS):
            q = chain * SLOTS + slot
            mixed = section_quad(arranged_ref, q, halves_ref[0, q], halves_ref[1, q]).astype(BF16)
            emit_halves(mixed, slot, upper, own_ref, send_ref)
        if chain == 0:
            edge = jnp.where(edge_lanes(0), halves_ref[0, 0], halves_ref[1, QUADS - 1])
            own_ref[SLOTS] = edge
            send_ref[SLOTS] = edge
    copies[3].wait()


def arrange_kernel(index, weights_ref, after_ref, arranged_ref, turned_ref):
    del after_ref
    arrange_section(weights_ref.at[index], arranged_ref, turned_ref)


def stage_kernel(level, index, chains, *refs):
    weights_ref, *kept_refs = refs[: 1 + chains]
    partial_ref, arranged_ref, turned_ref = refs[len(refs) - 3 :]
    upper = level_bit(level)
    turn_section(weights_ref if index is None else weights_ref.at[index], turned_ref)
    for q in range(QUADS):
        dense = dense_quad(turned_ref, q)
        low, high = [
            [dense[(2 * k + half) * RANK : (2 * k + half + 1) * RANK] for k in range(2)] for half in range(2)
        ]
        mine = [jnp.where(upper, second, first) for first, second in zip(low, high)]
        chain, slot = divmod(q, QUADS // chains)
        partial_ref[q] = half_dot(kept_refs[chain][slot], mine)
        for k in range(2):
            arranged_ref[q, k] = jnp.where(upper, low[k], high[k])


def arrive(partial_ref, arranged_ref, q, received):
    mixed = half_dot(received, [arranged_ref[q, 0], arranged_ref[q, 1]])
    return (mixed + partial_ref[q]).astype(BF16)


def meet_border(level, upper, kept, received, beside):
    inner = lax.axis_index("rows") & (2**level - 1)
    above = jnp.logical_and(jnp.logical_not(upper), inner == 2**level - 1)
    below = jnp.logical_and(upper, inner == 0)
    beside = jnp.where(jnp.logical_and(edge_lanes(0), above), received, beside)
    return jnp.where(jnp.logical_and(edge_lanes(3), below), received, beside)


def level_kernel(level, chain, merge, *refs):
    partial_ref, arranged_ref, received_ref = refs[:3]
    outputs = refs[len(refs) - (3 if chain == 0 else 2) :]
    own_ref, send_ref = outputs[:2]
    upper, next_upper = level_bit(level), level_bit(level + 1)
    for slot in range(SLOTS):
        q = chain * SLOTS + slot
        mixed = arrive(partial_ref, arranged_ref, q, received_ref[slot])
        emit_halves(mixed, q if merge else slot, next_upper, own_ref, send_ref)
    if chain == 0:
        kept, received = refs[3][SLOTS], received_ref[SLOTS]
        outputs[2][...] = meet_border(level, upper, kept, received, refs[4][...])
        theirs = jnp.logical_xor(edge_lanes(0), jnp.logical_not(upper))
        edge = jnp.where(theirs, received, kept)
        place = QUADS if merge else SLOTS
        own_ref[place] = edge
        send_ref[place] = edge


def near_sums(halves_ref, blocks_ref, near_ref, border_ref, arranged_ref, turned_ref):
    first_group, last_group = edge_lanes(0), edge_lanes(3)
    zeros = jnp.zeros((RHS, LANES), BF16)
    for half in range(2):
        lanes = slice(half * HALF, (half + 1) * HALF)
        for a in range(RANK):
            shifts = [blocks_ref[shift, a, :, lanes] for shift in (0, 1, 2, 0)]
            turned = jnp.concatenate(shifts, axis=0).T.astype(F32)
            turned_ref[a * PITCH : a * PITCH + LANES, :] = turned
        for q in range(QUADS):
            arranged_ref[q] = dense_quad(turned_ref, q)
        if half == 0:
            border_ref[0] = arranged_ref[0, RANK : 2 * RANK, :]
        else:
            border_ref[1] = arranged_ref[QUADS - 1, 2 * RANK : 3 * RANK, :]
        edge_before = zeros if half == 0 else halves_ref[0, QUADS - 1]
        edge_after = zeros if half == 1 else halves_ref[1, 0]
        for q in range(QUADS):
            centre = halves_ref[half, q]
            if q > 0:
                before = halves_ref[half, q - 1]
            else:
                final = halves_ref[half, QUADS - 1]
                before = pltpu.roll(jnp.where(last_group, edge_before, final), RANK, 1)
            if q < QUADS - 1:
                after = halves_ref[half, q + 1]
            else:
                first = halves_ref[half, 0]
                after = pltpu.roll(jnp.where(first_group, edge_after, first), LANES - RANK, 1)
            tiles = [
                diagonal_blocks(arranged_ref[q, shift * RANK : (shift + 1) * RANK, :], part)
                for shift in range(3)
                for part in range(4)
            ]
            matrix = jnp.concatenate(tiles, axis=0)
            stack = jnp.concatenate([centre, before, after], axis=1)
            near_ref[half, q] = jnp.dot(stack, matrix, preferred_element_type=F32)


def early_near_kernel(halves_ref, blocks_hbm, after_ref, near_ref, border_ref, blocks_ref, *scratch):
    del after_ref
    *scratch, sem = scratch

    @pl.when(lax.axis_index("rows") & 1 == 1)
    def _():
        copy = pltpu.make_async_copy(blocks_hbm, blocks_ref, sem)
        copy.start()
        copy.wait()
        near_sums(halves_ref, blocks_ref, near_ref, border_ref, *scratch)


def late_near_kernel(halves_ref, blocks_ref, near_in, border_in, after_ref, near_ref, border_ref, *scratch):
    del near_in, border_in, after_ref

    @pl.when(lax.axis_index("rows") & 1 == 0)
    def _():
        near_sums(halves_ref, blocks_ref, near_ref, border_ref, *scratch)


def border_term(border_ref, beside, half):
    zeros = jnp.zeros((RHS, LANES), BF16)
    if half == 0:
        edge = pltpu.roll(jnp.where(edge_lanes(3), beside, zeros), RANK, 1)
    else:
        edge = pltpu.roll(jnp.where(edge_lanes(0), beside, zeros), LANES - RANK, 1)
    tiles = [diagonal_blocks(border_ref[half], part) for part in range(4)]
    return jnp.dot(edge, jnp.concatenate(tiles, axis=0), preferred_element_type=F32)


def tail_kernel(
    level,
    partial_ref,
    last_ref,
    root_ref,
    kept_ref,
    received_ref,
    beside_ref,
    near_ref,
    border_ref,
    product_ref,
    coeffs_ref,
    rows_ref,
):
    for q in range(QUADS):
        coeffs_ref[q] = arrive(partial_ref, last_ref, q, received_ref[q])
    beside = meet_border(level, level_bit(level), kept_ref[QUADS], received_ref[QUADS], beside_ref[...])
    for q in range(QUADS):
        mixed = section_quad(root_ref, q, coeffs_ref[q, :, :LANES], coeffs_ref[q, :, LANES:])
        for half in range(2):
            total = mixed[:, half * LANES : (half + 1) * LANES] + near_ref[half, q]
            if q == half * (QUADS - 1):
                total = total + border_term(border_ref, beside, half)
            rows_ref[half, q * (RHS + 1) : q * (RHS + 1) + RHS, :] = total
    for half in range(2):
        lanes = slice(half * HALF, (half + 1) * HALF)
        for e in range(4):
            rows = [rows_ref[half, pl.ds(4 * d + e, QUADS, stride=RHS + 1), :] for d in range(4)]
            turned = jnp.concatenate(rows, axis=0).astype(BF16).T
            for row in (0, 16):
                blocks = [turned[g4 * RANK + row : g4 * RANK + row + 16, :] for g4 in range(4)]
                for d, block in enumerate(swap_lane_groups(blocks)):
                    product_ref[4 * d + e, row : row + 16, lanes] = block


VMEM_SPEC = pl.BlockSpec(memory_space=pltpu.VMEM)
ANY_SPEC = pl.BlockSpec(memory_space=pl.ANY)
HBM_SPEC = pl.BlockSpec(memory_space=pltpu.HBM)
TURNED = pltpu.VMEM((RANK * PITCH + LANES, LANES), F32)
ARRANGED = (QUADS, 2, 2 * RANK, LANES)
EDGE = jax.ShapeDtypeStruct((RHS, LANES), BF16)


def payload(chain, merge=False):
    slots = QUADS + 1 if merge else SLOTS + (chain == 0)
    return jax.ShapeDtypeStruct((slots, RHS, LANES), BF16)


def params(mib):
    return pltpu.CompilerParams(vmem_limit_bytes=mib * 2**20)


def in_hbm(array):
    return pltpu.with_memory_space_constraint(array, pltpu.HBM)


def arrange(factors, index, after):
    return pl.pallas_call(
        functools.partial(arrange_kernel, index),
        out_shape=jax.ShapeDtypeStruct(ARRANGED, BF16),
        in_specs=[VMEM_SPEC, ANY_SPEC],
        out_specs=VMEM_SPEC,
        scratch_shapes=[TURNED],
        compiler_params=params(16),
        cost_estimate=pl.CostEstimate(flops=2 * 10**6, bytes_accessed=2 * 2**20, transcendentals=0),
        name="arrange",
    )(factors, after)


def stage(level, weights, index, kept, after):
    return pl.pallas_call(
        functools.partial(stage_kernel, level, index, len(kept)),
        out_shape=(
            jax.ShapeDtypeStruct((QUADS, RHS, 2 * LANES), F32),
            jax.ShapeDtypeStruct((QUADS, 2, RANK, LANES), BF16),
        ),
        in_specs=[VMEM_SPEC] * (1 + len(kept)) + [ANY_SPEC],
        out_specs=(VMEM_SPEC, VMEM_SPEC),
        scratch_shapes=[TURNED],
        compiler_params=params(16),
        cost_estimate=pl.CostEstimate(flops=2 * 10**6, bytes_accessed=2 * 2**20, transcendentals=0),
        name="stage",
    )(weights, *kept, after)


def head(vectors, factors):
    section = (2 * RANK, 2 * RANK, HALF)
    outs = [payload(chain) for chain in range(CHAINS) for _ in range(2)]
    outs += [jax.ShapeDtypeStruct((2, QUADS, RHS, LANES), BF16), jax.ShapeDtypeStruct(section, BF16)]
    *pairs, halves, section_1 = pl.pallas_call(
        head_kernel,
        out_shape=tuple(outs),
        in_specs=[HBM_SPEC, HBM_SPEC],
        out_specs=(VMEM_SPEC,) * len(outs),
        scratch_shapes=[
            pltpu.VMEM((2, RHS, RANK, HALF), BF16),
            pltpu.VMEM(section, BF16),
            pltpu.VMEM((2, RHS * (QUADS + 1) + QUADS, LANES), F32),
            TURNED,
            pltpu.VMEM(ARRANGED, BF16),
            pltpu.SemaphoreType.DMA((4,)),
        ],
        compiler_params=params(14),
        name="head",
    )(in_hbm(vectors), in_hbm(factors))
    return pairs[::2], pairs[1::2], halves, section_1


def level_step(level, chain, partial, arranged, kept, received, beside, into=None, after=()):
    merge = into is not None
    edges = [kept, beside] if chain == 0 else []
    filled = list(into) if merge and chain > 0 else []
    outs = [payload(chain, merge)] * 2 + [EDGE] * (chain == 0)
    return pl.pallas_call(
        functools.partial(level_kernel, level, chain, merge),
        out_shape=tuple(outs),
        in_specs=[VMEM_SPEC] * (3 + len(edges) + len(filled)) + [ANY_SPEC] * len(after),
        out_specs=(VMEM_SPEC,) * len(outs),
        input_output_aliases={3: 0, 4: 1} if filled else {},
        compiler_params=params(6),
        name="level",
    )(partial, arranged, received, *edges, *filled, *after)


def near_field(halves, neighbor_blocks, after, filled=()):
    early = not filled
    scratch = [pltpu.VMEM((QUADS, LANES, LANES), BF16), TURNED]
    if early:
        scratch = [pltpu.VMEM(neighbor_blocks.shape, BF16), *scratch, pltpu.SemaphoreType.DMA(())]
    return pl.pallas_call(
        early_near_kernel if early else late_near_kernel,
        out_shape=(
            jax.ShapeDtypeStruct((2, QUADS, RHS, LANES), F32),
            jax.ShapeDtypeStruct((2, RANK, LANES), BF16),
        ),
        in_specs=[VMEM_SPEC, HBM_SPEC if early else VMEM_SPEC] + [VMEM_SPEC] * len(filled) + [ANY_SPEC],
        out_specs=(VMEM_SPEC, VMEM_SPEC),
        input_output_aliases={} if early else {2: 0, 3: 1},
        scratch_shapes=scratch,
        compiler_params=params(12),
        cost_estimate=pl.CostEstimate(flops=4 * 10**6, bytes_accessed=3 * 2**20, transcendentals=0),
        name="near",
    )(halves, in_hbm(neighbor_blocks) if early else neighbor_blocks, *filled, after)


def tail(level, *operands):
    return pl.pallas_call(
        functools.partial(tail_kernel, level),
        out_shape=jax.ShapeDtypeStruct((RHS, RANK, 2 * HALF), BF16),
        in_specs=[VMEM_SPEC] * len(operands),
        out_specs=VMEM_SPEC,
        scratch_shapes=[
            pltpu.VMEM((QUADS, RHS, 2 * LANES), BF16),
            pltpu.VMEM((2, QUADS * (RHS + 1) + RHS, LANES), F32),
        ],
        compiler_params=params(12),
        name="tail",
    )(*operands)


def shards(vectors, factors, neighbor_blocks):
    level_count = factors.shape[0] - 2
    count = lax.axis_size("rows")
    kept, sending, halves, section_1 = head(vectors, factors)
    sending[0], factors = lax.optimization_barrier((sending[0], factors))
    beside = jnp.zeros(EDGE.shape, EDGE.dtype)
    for level in range(level_count - 1):
        partners = [(i, i ^ (1 << level)) for i in range(count)]
        received = [lax.ppermute(part, "rows", partners) for part in sending]
        if level == 0:
            staged = stage(level, section_1, None, kept, sending[-1])
        else:
            staged = stage(level, factors, level + 1, kept, sending[-1])
        into = () if level == level_count - 2 else None
        after = ()
        if level == 0:
            filled = near_field(halves, neighbor_blocks, staged[0])
            after = filled[:1]
        for chain in range(CHAINS):
            outs = level_step(level, chain, *staged, kept[chain], received[chain], beside, into, after)
            kept[chain], sending[chain] = outs[:2]
            if chain == 0:
                beside = outs[2]
            if into is not None:
                into = outs[:2]
    level = level_count - 1
    kept, sending = into
    received = lax.ppermute(sending, "rows", [(i, i ^ (1 << level)) for i in range(count)])
    near, border = near_field(halves, neighbor_blocks, sending, filled)
    partial, last = stage(level, factors, level + 1, [kept], sending)
    root = arrange(factors, level + 2, sending)
    return tail(level, partial, last, root, kept, received, beside, near, border)


def solution(mesh):
    placed = (P(None, None, "rows"), P(None, None, None, "rows"), P(None, None, None, "rows"))
    return jax.shard_map(
        shards, mesh=mesh, in_specs=placed, out_specs=P(None, None, "rows"), check_vma=False
    )
```
